32 devices in a mesh: cp: 8 (over z, x), grp: 4 (over y, core).
Axes of the slice: x: 2, y: 2, z: 4, core: 2. Of those that a mesh axis runs over, the one named last changes fastest.
Arguments:
- queries: bfloat16 [8192, 8192], P(('cp', 'grp')), may hold values from -60 to 60
- keys: bfloat16 [8192, 1024], P(('cp', 'grp')), may hold values from -4 to 4
- values: bfloat16 [8192, 1024], P(('cp', 'grp')), may hold values from -6 to 6
- doc_lengths: int32 [8, 3], P('cp'), may hold values from 1 to 768, 1024 in all within a row
- send_tile: int32 [32, 16], P(('cp', 'grp')), may hold values from 0 to 8, as said below
- take_slot: int32 [32, 8], P(('cp', 'grp')), may hold values from 0 to 15, as said below
Outputs:
- attended: bfloat16 [8192, 8192], P(('cp', 'grp'))
The draws below stay inside these ranges and needn't reach their ends.
Inputs may be any that keep to these rules, and one draw needn't show every extreme that they name: `send_tile`: entry c2 * 2 + s of row d = c * 4 + g names the arrival tile (0 to 7) that device (c, g) sends in slot s to device (c2, g), and 8 marks an empty slot. Every tile of a device is sent exactly once; each device sends 2 tiles to each of exactly 4 peers and none to the others. `take_slot`: row d2 lists, for each owner tile of device d2, the received slot c * 2 + s (slot s of the tiles sent by device (c, g) of the same g) that fills it; every filled send slot fills exactly one owner tile, so each device receives from exactly 4 peers.
All inputs are finite; a program needn't handle non-finite values.
Results may differ from the reference program's by a relative error of at most 0.0037.
Values may be sent and summed in bfloat16 or wider, within the bound.
A program may use at most 128 MiB of HBM per device.

```python
import math
import jax
import jax.numpy as jnp
import numpy as np
from jax import lax

QUERY_HEADS = 64
KEY_VALUE_HEADS = 8
HEAD_SIZE = 128
TOK_DEV = 256
DOCS = 3
SLOTS = 2
WINDOW_TOKENS = 8192
N_CP = 8
N_GRP = 4


def key_field(key):
    unscaled_scores = jnp.clip(jax.random.normal(jax.random.fold_in(key, 101), (WINDOW_TOKENS, KEY_VALUE_HEADS * HEAD_SIZE), jnp.float32), -4.0, 4.0)
    return unscaled_scores


def draw_keys(key, part):
    return key_field(key).astype(jnp.bfloat16)


def draw_queries(key, part):
    unscaled_scores = jnp.clip(jax.random.normal(jax.random.fold_in(key, 103), (WINDOW_TOKENS, QUERY_HEADS * HEAD_SIZE), jnp.float32), -4.0, 4.0)
    return unscaled_scores.astype(jnp.bfloat16)


def placement(key):
    base = jax.random.fold_in(key, 7)
    device_count = N_CP * N_GRP
    half_peers = N_CP // 2
    group_keys = jax.random.split(jax.random.fold_in(base, 1), N_GRP)
    offsets = jax.vmap(lambda item: jax.random.permutation(item, N_CP)[:half_peers])(group_keys).astype(jnp.int32)
    tile_keys = jax.random.split(jax.random.fold_in(base, 2), device_count)
    tile_order = jax.vmap(lambda item: jax.random.permutation(item, N_CP))(tile_keys).astype(jnp.int32)
    fill_keys = jax.random.split(jax.random.fold_in(base, 3), device_count)
    shuffle = jax.vmap(lambda item: jax.random.permutation(item, N_CP))(fill_keys).astype(jnp.int32)
    device_ids = jnp.arange(device_count, dtype=jnp.int32)
    cp_index = device_ids // N_GRP
    grp_index = device_ids % N_GRP
    device_offsets = offsets[grp_index]
    peer_index = (cp_index[:, None] + device_offsets) % N_CP
    sending = jnp.full((device_count, N_CP, SLOTS), N_CP, jnp.int32)
    sending = sending.at[device_ids[:, None], peer_index].set(tile_order.reshape(device_count, half_peers, SLOTS))
    source_cp = (cp_index[:, None] - device_offsets) % N_CP
    received = source_cp[:, :, None] * SLOTS + jnp.arange(SLOTS, dtype=jnp.int32)[None, None, :]
    taking = jnp.take_along_axis(received.reshape(device_count, N_CP), shuffle, axis=1)
    return (sending.reshape(device_count, N_CP * SLOTS).astype(jnp.int32), taking.astype(jnp.int32))


def draw_send_tile(key, part):
    return placement(key)[0]


def draw_take_slot(key, part):
    return placement(key)[1]


def steps_of(stream_key, shape, cuts, least, high):
    factor_of = 1.0
    for dim, parts in cuts:
        draws = jax.random.uniform(jax.random.fold_in(jax.random.fold_in(stream_key, 6), dim), (parts,), jnp.float32, least / len(cuts), high / len(cuts))
        factor_of = factor_of * jnp.repeat(jnp.exp(draws), shape[dim] // parts).reshape((-1,) + (1,) * (len(shape) - 1 - dim))
    return factor_of


def profile(number_of, total, most, lean):
    portions = [(1 << 20) // math.isqrt(rank ** lean) + 1 for rank in range(2, number_of + 1)]
    rest, given = total - most - (number_of - 1), [1] * (number_of - 1)
    while rest > 0:
        movable = [i for i in range(number_of - 1) if given[i] < most]
        pool, left = sum([portions[i] for i in movable]), rest
        for i in movable:
            more = min(most - given[i], max(1, left * portions[i] // pool), rest)
            given[i] = given[i] + more
            rest = rest - more
    return np.array([most] + given)


def ragged(key, amount, total, bound, skew):
    if amount == 2:
        one = jax.random.randint(key, (), max(1, total - bound), min(bound, total - 1) + 1)
        return jnp.stack([one, total - one])
    sizes = jnp.asarray(profile(amount, total, bound, skew), jnp.int32)
    twos = (amount - 1) // 2
    source_of, sink = sizes[1:1 + 2 * twos:2], sizes[2:2 + 2 * twos:2]
    margin = jnp.minimum(source_of - 1, bound - sink)
    shifted = jax.random.randint(jax.random.fold_in(key, 1), (twos,), 0, 1 << 20) % (margin + 1)
    sizes = sizes.at[1:1 + 2 * twos:2].set(source_of - shifted).at[2:2 + 2 * twos:2].set(sink + shifted)
    return sizes[jax.random.permutation(jax.random.fold_in(key, 2), amount)]


def gaussian(rng, shape, width, reach, cuts=(), kind=jnp.bfloat16):
    values = width * jax.random.normal(rng, shape, jnp.float32)
    if cuts:
        values = values * steps_of(rng, shape, cuts, -0.22, 0.18)
    return jnp.clip(values, -reach, reach).astype(kind)


def setup_inputs(seed: int = 0) -> dict:
    seeds = jax.random.split(jax.random.key(seed), 7)
    return {
        "queries": draw_queries(jax.random.fold_in(seeds[6], 71), 0),
        "keys": draw_keys(jax.random.fold_in(seeds[6], 71), 0),
        "values": gaussian(seeds[2], (WINDOW_TOKENS, KEY_VALUE_HEADS * HEAD_SIZE), 1.0, 6.0, ((0, 32),)),
        "doc_lengths": jax.vmap(lambda own: ragged(own, DOCS, N_GRP * TOK_DEV, N_GRP * TOK_DEV - N_GRP * TOK_DEV // 4, 2))(jax.random.split(seeds[3], N_CP)).reshape((N_CP, DOCS)).astype(jnp.int32),
        "send_tile": draw_send_tile(jax.random.fold_in(seeds[6], 71), 0),
        "take_slot": draw_take_slot(jax.random.fold_in(seeds[6], 71), 0),
    }


def owner_rows(send_tile, take_slot):
    device_count = N_CP * N_GRP
    tile_rows = TOK_DEV // N_CP
    device_ids = jnp.arange(device_count, dtype=jnp.int32)
    cp_index = device_ids // N_GRP
    grp_index = device_ids % N_GRP
    source_cp = take_slot // SLOTS
    source_slot = take_slot % SLOTS
    source_dev = source_cp * N_GRP + grp_index[:, None]
    column = cp_index[:, None] * SLOTS + source_slot
    arrival_tile = send_tile[source_dev, column]
    start = (source_dev * N_CP + arrival_tile) * tile_rows
    offsets = jnp.arange(tile_rows, dtype=jnp.int32)
    return (start[:, :, None] + offsets[None, None, :]).reshape(-1).astype(jnp.int32)

def attend(query_rows, key_rows, value_rows, query_pos, key_pos, query_doc, key_doc):
    queries_per_group = QUERY_HEADS // KEY_VALUE_HEADS
    score_scale = 1.0 / math.sqrt(HEAD_SIZE)
    allowed = (query_doc[:, None] == key_doc[None, :]) & (key_pos[None, :] <= query_pos[:, None])
    pieces = []
    for head_number_index in range(KEY_VALUE_HEADS):
        query_head = query_rows[:, head_number_index * queries_per_group * HEAD_SIZE:(head_number_index + 1) * queries_per_group * HEAD_SIZE]
        query_head = query_head.reshape(-1, queries_per_group, HEAD_SIZE).astype(jnp.float32)
        key_head = key_rows[:, head_number_index * HEAD_SIZE:(head_number_index + 1) * HEAD_SIZE].astype(jnp.float32)
        value_head = value_rows[:, head_number_index * HEAD_SIZE:(head_number_index + 1) * HEAD_SIZE].astype(jnp.float32)
        scores = jnp.einsum('qgd,kd->gqk', query_head, key_head) * score_scale
        scores = jnp.where(allowed[None], scores, -jnp.inf)
        row_max = lax.optimization_barrier(jnp.max(scores, axis=2, keepdims=True))
        weights = jnp.exp(scores - row_max)
        totals = lax.optimization_barrier(jnp.sum(weights, axis=2))
        rounded = lax.optimization_barrier(weights.astype(jnp.bfloat16)).astype(jnp.float32)
        summed = jnp.einsum('gqk,kd->qgd', rounded, value_head)
        mixed = summed / jnp.transpose(totals)[:, :, None]
        pieces.append(mixed.reshape(-1, queries_per_group * HEAD_SIZE))
    return jnp.concatenate(pieces, axis=1).astype(jnp.bfloat16)

def reference(queries, keys, values, doc_lengths, send_tile, take_slot):
    sorted_ordering = owner_rows(send_tile, take_slot)
    group_length = N_GRP * TOK_DEV
    owned_queries = jnp.take(queries, sorted_ordering, axis=0).reshape(N_CP, group_length, QUERY_HEADS * HEAD_SIZE)
    holder_keys = jnp.take(keys, sorted_ordering, axis=0).reshape(N_CP, group_length, KEY_VALUE_HEADS * HEAD_SIZE)
    holder_values = jnp.take(values, sorted_ordering, axis=0).reshape(N_CP, group_length, KEY_VALUE_HEADS * HEAD_SIZE)

    def one_group(inputs):
        group_queries, group_keys, group_values, lengths = inputs
        doc_ends = jnp.cumsum(lengths.astype(jnp.int32)).astype(jnp.int32)
        positions = jnp.arange(group_length, dtype=jnp.int32)
        doc_index = lax.optimization_barrier(jnp.sum((positions[:, None] >= doc_ends[None, :]).astype(jnp.int32), axis=1))
        outputs = []
        for block_index in range(N_GRP):
            first_row = block_index * TOK_DEV
            last_row = first_row + TOK_DEV
            outputs.append(attend(group_queries[first_row:last_row], group_keys[:last_row], group_values[:last_row], positions[first_row:last_row], positions[:last_row], doc_index[first_row:last_row], doc_index[:last_row]))
        return jnp.concatenate(outputs, axis=0)
    attended = lax.map(one_group, (owned_queries, holder_keys, holder_values, doc_lengths))
    return attended.reshape(WINDOW_TOKENS, QUERY_HEADS * HEAD_SIZE)
```

```python
import functools
import math

import jax
import jax.numpy as jnp
from jax import lax
from jax.experimental import pallas as pl
from jax.experimental.pallas import tpu as pltpu
from jax.sharding import PartitionSpec as P

QUERY_HEADS = 64
KEY_VALUE_HEADS = 8
HEAD_SIZE = 128
PER_GROUP = QUERY_HEADS // KEY_VALUE_HEADS
HEAD_WIDTH = PER_GROUP * HEAD_SIZE
CHUNKS = 4


def pack_kernel(chosen_ref, *refs, tiles, slots, spans):
    count = len(spans)
    sources, targets, sems = refs[: len(refs) - 1 - count], refs[-1 - count : -1], refs[-1]

    def each(act):
        def one(slot, carry):
            tile = chosen_ref[slot]

            @pl.when(tile < tiles)
            def _():
                for number, (source, start, width) in enumerate(spans):
                    piece = sources[source].at[tile, :, pl.ds(start, width)]
                    act(pltpu.make_async_copy(piece, targets[number].at[slot], sems.at[number, slot]))

            return carry

        lax.fori_loop(0, slots, one, 0)

    each(lambda copy: copy.start())
    each(lambda copy: copy.wait())


def pack(chosen, arrays, spans, tile_rows):
    tiles, slots = arrays[0].shape[0] // tile_rows, chosen.shape[0]
    tiled = [a.reshape(tiles, tile_rows, a.shape[1]) for a in arrays]
    any_spec = pl.BlockSpec(memory_space=pl.ANY)
    return pl.pallas_call(
        functools.partial(pack_kernel, tiles=tiles, slots=slots, spans=spans),
        out_shape=[jax.ShapeDtypeStruct((slots, tile_rows, w), jnp.bfloat16) for _, _, w in spans],
        grid_spec=pltpu.PrefetchScalarGridSpec(
            num_scalar_prefetch=1,
            grid=(1,),
            in_specs=[any_spec] * len(tiled),
            out_specs=[any_spec] * len(spans),
            scratch_shapes=[pltpu.SemaphoreType.DMA((len(spans), slots))],
        ),
    )(chosen, *tiled)


def attend_kernel(take_ref, lengths_ref, info_ref, *refs, tiles, docs):
    pieces = refs[:tiles]
    key_ref, value_ref = refs[tiles : tiles + 2]
    out_ref, bias_ref = refs[-2], refs[-1]
    rows, length = bias_ref.shape

    @pl.when(pl.program_id(0) == 0)
    def _():
        spot = info_ref[0] + lax.broadcasted_iota(jnp.int32, (rows, 1), 0)
        begin = jnp.zeros((rows, 1), jnp.int32)
        end = 0
        for k in range(docs):
            end = end + lengths_ref[k]
            begin = jnp.where(spot >= end, end, begin)
        column = lax.broadcasted_iota(jnp.int32, (rows, length), 1)
        bias_ref[...] = jnp.where((column >= begin) & (column <= spot), 0.0, -jnp.inf)

    keys, values = key_ref[...], value_ref[...]
    factor = math.log2(math.e) / math.sqrt(HEAD_SIZE)
    for head in range(PER_GROUP):
        span = slice(head * HEAD_SIZE, (head + 1) * HEAD_SIZE)
        query = jnp.concatenate([p[0, :, span] for p in pieces], axis=0)
        scores = lax.dot_general(
            query, keys, (((1,), (1,)), ((), ())), preferred_element_type=jnp.float32
        )
        scores = scores + bias_ref[...]
        top = jnp.max(scores, axis=1, keepdims=True)
        weights = jnp.exp2((scores - top) * factor)
        totals = jnp.sum(weights, axis=1, keepdims=True)
        summed = jnp.dot(weights.astype(jnp.bfloat16), values, preferred_element_type=jnp.float32)
        out_ref[:, span] = (summed / totals).astype(jnp.bfloat16)


def attend(take, lengths, info, got, keys, values, result, first):
    tiles, (_, tile_rows, width) = take.shape[0], got.shape
    rows, length = tiles * tile_rows, keys.shape[0]
    heads = width // HEAD_WIDTH
    in_specs = [
        pl.BlockSpec((1, tile_rows, HEAD_WIDTH), lambda h, t, e, n, i=i: (t[i], 0, h))
        for i in range(tiles)
    ]
    in_specs += [pl.BlockSpec((length, HEAD_SIZE), lambda h, t, e, n: (0, first + h))] * 2
    operands = [got] * tiles + [keys, values]
    aliases = {}
    if result is not None:
        in_specs.append(pl.BlockSpec(memory_space=pl.ANY))
        aliases = {3 + len(operands): 0}
        operands.append(result)
    pairs = heads * PER_GROUP * rows * length
    return pl.pallas_call(
        functools.partial(attend_kernel, tiles=tiles, docs=lengths.shape[0]),
        out_shape=jax.ShapeDtypeStruct((rows, QUERY_HEADS * HEAD_SIZE), jnp.bfloat16),
        grid_spec=pltpu.PrefetchScalarGridSpec(
            num_scalar_prefetch=3,
            grid=(heads,),
            in_specs=in_specs,
            out_specs=pl.BlockSpec((rows, HEAD_WIDTH), lambda h, t, e, n: (0, first + h)),
            scratch_shapes=[pltpu.VMEM((rows, length), jnp.float32)],
        ),
        input_output_aliases=aliases,
        compiler_params=pltpu.CompilerParams(vmem_limit_bytes=40 * 2**20),
        cost_estimate=pl.CostEstimate(
            flops=4 * pairs * HEAD_SIZE, bytes_accessed=2 * rows * width * 2, transcendentals=pairs
        ),
    )(take, lengths, info, *operands)


def local(queries, keys, values, doc_lengths, send_tile, take_slot):
    tok_rows = queries.shape[0]
    peer_count = lax.axis_size("cp")
    tile_rows = tok_rows // peer_count
    chosen, placed = send_tile[0], take_slot[0]
    kv_width = KEY_VALUE_HEADS * HEAD_SIZE
    q_width = QUERY_HEADS * HEAD_SIZE // CHUNKS
    spans = [(1, 0, kv_width), (2, 0, kv_width)]
    spans += [(0, i * q_width, q_width) for i in range(CHUNKS)]
    sent = pack(chosen, [queries, keys, values], spans, tile_rows)

    def exchange(source):
        return lax.all_to_all(source, "cp", split_axis=0, concat_axis=0, tiled=True)

    def share(source):
        got = exchange(source).reshape(-1, kv_width)
        (own,) = pack(placed, [got], [(0, 0, kv_width)], tile_rows)
        return lax.all_gather(own.reshape(tok_rows, kv_width), "grp", axis=0, tiled=True)

    all_keys, all_values = share(sent[0]), share(sent[1])
    lengths = doc_lengths[0]
    info = (lax.axis_index("grp") * tok_rows).astype(jnp.int32).reshape(1)
    result = None
    for i in range(CHUNKS):
        got = exchange(sent[2 + i])
        first = i * (KEY_VALUE_HEADS // CHUNKS)
        result = attend(placed, lengths, info, got, all_keys, all_values, result, first)
    return result


def solution(mesh):
    both = P(("cp", "grp"), None)
    return jax.shard_map(
        local,
        mesh=mesh,
        in_specs=(both, both, both, P("cp", None), both, both),
        out_specs=both,
        check_vma=False,
    )
```

```python
import functools
import math

import jax
import jax.numpy as jnp
from jax import lax
from jax.experimental import pallas as pl
from jax.experimental.pallas import tpu as pltpu
from jax.sharding import PartitionSpec as P

QUERY_HEADS = 64
KEY_VALUE_HEADS = 8
HEAD_SIZE = 128
PER_GROUP = QUERY_HEADS // KEY_VALUE_HEADS
HEAD_WIDTH = PER_GROUP * HEAD_SIZE
PARTS = (6, 2)


def pack_kernel(chosen_ref, *refs, tiles, slots, count):
    sources, target, sems = refs[:count], refs[count], refs[count + 1]
    step = pl.program_id(0)
    width = sources[0].shape[2]

    def each(act):
        def one(slot, carry):
            tile = chosen_ref[slot]

            @pl.when(tile < tiles)
            def _():
                for i, source in enumerate(sources):
                    start = pl.multiple_of((step * count + i) * width, width)
                    place = target.at[slot, :, pl.ds(start, width)]
                    act(pltpu.make_async_copy(source.at[tile], place, sems.at[i, slot]))

            return carry

        lax.fori_loop(0, slots, one, 0)

    each(lambda copy: copy.start())
    each(lambda copy: copy.wait())


def pack(chosen, sources, tile_rows, width, first, steps):
    tiles, slots, count = sources[0].shape[0] // tile_rows, chosen.shape[0], len(sources)
    tiled = [a.reshape(tiles, tile_rows, a.shape[1]) for a in sources]
    out_width = steps * count * width
    return pl.pallas_call(
        functools.partial(pack_kernel, tiles=tiles, slots=slots, count=count),
        out_shape=jax.ShapeDtypeStruct((slots, tile_rows, out_width), jnp.bfloat16),
        grid_spec=pltpu.PrefetchScalarGridSpec(
            num_scalar_prefetch=1,
            grid=(steps,),
            in_specs=[pl.BlockSpec((tiles, tile_rows, width), lambda j, c: (0, 0, first + j))] * count,
            out_specs=pl.BlockSpec(memory_space=pl.ANY),
            scratch_shapes=[pltpu.SemaphoreType.DMA((count, slots))],
        ),
        compiler_params=pltpu.CompilerParams(vmem_limit_bytes=40 * 2**20),
        cost_estimate=pl.CostEstimate(
            flops=0, bytes_accessed=4 * tiles * tile_rows * out_width, transcendentals=0
        ),
    )(chosen, *tiled)


def attend_kernel(take_ref, lengths_ref, info_ref, *refs, tiles, docs):
    pieces = refs[:tiles]
    key_ref, value_ref = refs[tiles : tiles + 2]
    out_ref, bias_ref = refs[-2], refs[-1]
    rows, length = bias_ref.shape

    @pl.when(pl.program_id(0) == 0)
    def _():
        spot = info_ref[0] + lax.broadcasted_iota(jnp.int32, (rows, 1), 0)
        begin = jnp.zeros((rows, 1), jnp.int32)
        end = 0
        for k in range(docs):
            end = end + lengths_ref[k]
            begin = jnp.where(spot >= end, end, begin)
        column = lax.broadcasted_iota(jnp.int32, (rows, length), 1)
        bias_ref[...] = jnp.where((column >= begin) & (column <= spot), 0.0, -jnp.inf)

    keys, values = key_ref[...], value_ref[...]
    factor = math.log2(math.e) / math.sqrt(HEAD_SIZE)
    for head in range(PER_GROUP):
        span = slice(head * HEAD_SIZE, (head + 1) * HEAD_SIZE)
        query = jnp.concatenate([p[0, :, span] for p in pieces], axis=0)
        scores = lax.dot_general(
            query, keys, (((1,), (1,)), ((), ())), preferred_element_type=jnp.float32
        )
        scores = scores + bias_ref[...]
        top = jnp.max(scores, axis=1, keepdims=True)
        weights = jnp.exp2((scores - top) * factor)
        totals = jnp.sum(weights, axis=1, keepdims=True)
        summed = jnp.dot(weights.astype(jnp.bfloat16), values, preferred_element_type=jnp.float32)
        out_ref[:, span] = (summed / totals).astype(jnp.bfloat16)


def attend(take, lengths, info, got, shared, result, first):
    tiles, (_, tile_rows, width) = take.shape[0], got.shape
    rows, length = tiles * tile_rows, shared.shape[0]
    heads = width // HEAD_WIDTH
    in_specs = [
        pl.BlockSpec((1, tile_rows, HEAD_WIDTH), lambda h, t, e, n, i=i: (t[i], 0, h))
        for i in range(tiles)
    ]
    in_specs += [
        pl.BlockSpec((length, HEAD_SIZE), lambda h, t, e, n, b=b: (0, b + first + h))
        for b in (0, KEY_VALUE_HEADS)
    ]
    operands = [got] * tiles + [shared, shared]
    aliases = {}
    if result is not None:
        in_specs.append(pl.BlockSpec(memory_space=pl.ANY))
        aliases = {3 + len(operands): 0}
        operands.append(result)
    pairs = heads * PER_GROUP * rows * length
    return pl.pallas_call(
        functools.partial(attend_kernel, tiles=tiles, docs=lengths.shape[0]),
        out_shape=jax.ShapeDtypeStruct((rows, QUERY_HEADS * HEAD_SIZE), jnp.bfloat16),
        grid_spec=pltpu.PrefetchScalarGridSpec(
            num_scalar_prefetch=3,
            grid=(heads,),
            in_specs=in_specs,
            out_specs=pl.BlockSpec((rows, HEAD_WIDTH), lambda h, t, e, n: (0, first + h)),
            scratch_shapes=[pltpu.VMEM((rows, length), jnp.float32)],
        ),
        input_output_aliases=aliases,
        compiler_params=pltpu.CompilerParams(vmem_limit_bytes=40 * 2**20),
        cost_estimate=pl.CostEstimate(
            flops=4 * pairs * HEAD_SIZE, bytes_accessed=2 * rows * width * 2, transcendentals=pairs
        ),
    )(take, lengths, info, *operands)


def local(queries, keys, values, doc_lengths, send_tile, take_slot):
    tok_rows = queries.shape[0]
    peer_count = lax.axis_size("cp")
    tile_rows = tok_rows // peer_count
    chosen, placed = send_tile[0], take_slot[0]
    kv_width = KEY_VALUE_HEADS * HEAD_SIZE

    def exchange(source):
        return lax.all_to_all(source, "cp", split_axis=0, concat_axis=0, tiled=True)

    info = (lax.axis_index("grp") * tok_rows).astype(jnp.int32).reshape(1)
    got = exchange(pack(chosen, [keys, values], tile_rows, kv_width, 0, 1))
    owned, shared = got.reshape(-1, 2 * kv_width), None
    result, first = None, 0
    for heads in PARTS:
        packed = pack(chosen, [queries], tile_rows, HEAD_WIDTH, first, heads)
        packed, got = lax.optimization_barrier((packed, got))
        got = exchange(packed)
        if shared is None:
            owned = pack(placed, [owned], tile_rows, 2 * kv_width, 0, 1)
            shared = lax.all_gather(owned.reshape(tok_rows, 2 * kv_width), "grp", axis=0, tiled=True)
        result = attend(placed, doc_lengths[0], info, got, shared, result, first)
        first += heads
    return result


def solution(mesh):
    both = P(("cp", "grp"), None)
    return jax.shard_map(
        local,
        mesh=mesh,
        in_specs=(both, both, both, P("cp", None), both, both),
        out_specs=both,
        check_vma=False,
    )
```

```python
import functools
import math

import jax
import jax.numpy as jnp
from jax import lax
from jax.experimental import pallas as pl
from jax.experimental.pallas import tpu as pltpu
from jax.sharding import PartitionSpec as P

QUERY_HEADS = 64
KEY_VALUE_HEADS = 8
HEAD_SIZE = 128
PER_GROUP = QUERY_HEADS // KEY_VALUE_HEADS
HEAD_WIDTH = PER_GROUP * HEAD_SIZE
PARTS = (6, 2)


def pack_kernel(chosen_ref, *refs, tiles, slots, count):
    sources, target, sems = refs[:count], refs[count], refs[count + 1]
    width = sources[0].shape[2]

    def each(act):
        def one(slot, carry):
            tile = chosen_ref[slot]

            @pl.when(tile < tiles)
            def _():
                for i, source in enumerate(sources):
                    place = target.at[slot, :, pl.ds(i * width, width)]
                    act(pltpu.make_async_copy(source.at[tile], place, sems.at[i, slot]))

            return carry

        lax.fori_loop(0, slots, one, 0)

    each(lambda copy: copy.start())
    each(lambda copy: copy.wait())


def pack(chosen, sources, blocks, tile_rows, width):
    tiles, slots, count = sources[0].shape[0] // tile_rows, chosen.shape[0], len(sources)
    tiled = [a.reshape(tiles, tile_rows, a.shape[1]) for a in sources]
    out_width = count * width
    return pl.pallas_call(
        functools.partial(pack_kernel, tiles=tiles, slots=slots, count=count),
        out_shape=jax.ShapeDtypeStruct((slots, tile_rows, out_width), jnp.bfloat16),
        grid_spec=pltpu.PrefetchScalarGridSpec(
            num_scalar_prefetch=1,
            grid=(1,),
            in_specs=[
                pl.BlockSpec((tiles, tile_rows, width), lambda j, c, b=b: (0, 0, b)) for b in blocks
            ],
            out_specs=pl.BlockSpec(memory_space=pl.ANY),
            scratch_shapes=[pltpu.SemaphoreType.DMA((count, slots))],
        ),
        compiler_params=pltpu.CompilerParams(vmem_limit_bytes=40 * 2**20),
        cost_estimate=pl.CostEstimate(
            flops=0, bytes_accessed=4 * tiles * tile_rows * out_width, transcendentals=0
        ),
    )(chosen, *tiled)


def attend_kernel(take_ref, lengths_ref, info_ref, *refs, tiles, docs):
    pieces = refs[:tiles]
    key_ref, value_ref = refs[tiles : tiles + 2]
    out_ref, bias_ref = refs[-2], refs[-1]
    rows, length = bias_ref.shape

    @pl.when(pl.program_id(0) == 0)
    def _():
        spot = info_ref[0] + lax.broadcasted_iota(jnp.int32, (rows, 1), 0)
        begin = jnp.zeros((rows, 1), jnp.int32)
        end = 0
        for k in range(docs):
            end = end + lengths_ref[k]
            begin = jnp.where(spot >= end, end, begin)
        column = lax.broadcasted_iota(jnp.int32, (rows, length), 1)
        bias_ref[...] = jnp.where((column >= begin) & (column <= spot), 0.0, -jnp.inf)

    keys, values = key_ref[...], value_ref[...]
    factor = math.log2(math.e) / math.sqrt(HEAD_SIZE)
    for head in range(PER_GROUP):
        span = slice(head * HEAD_SIZE, (head + 1) * HEAD_SIZE)
        query = jnp.concatenate([p[0, :, span] for p in pieces], axis=0)
        scores = lax.dot_general(
            query, keys, (((1,), (1,)), ((), ())), preferred_element_type=jnp.float32
        )
        scores = scores + bias_ref[...]
        top = jnp.max(scores, axis=1, keepdims=True)
        weights = jnp.exp2((scores - top) * factor)
        totals = jnp.sum(weights, axis=1, keepdims=True)
        summed = jnp.dot(weights.astype(jnp.bfloat16), values, preferred_element_type=jnp.float32)
        out_ref[:, span] = (summed / totals).astype(jnp.bfloat16)


def attend(take, lengths, info, got, shared, result, first, heads, skip):
    tiles, tile_rows = take.shape[0], got.shape[1]
    rows, length = tiles * tile_rows, shared.shape[0]
    in_specs = [
        pl.BlockSpec((1, tile_rows, HEAD_WIDTH), lambda h, t, e, n, i=i: (t[i], 0, skip + h))
        for i in range(tiles)
    ]
    in_specs += [
        pl.BlockSpec((length, HEAD_SIZE), lambda h, t, e, n, b=b: (0, b + first + h))
        for b in (0, KEY_VALUE_HEADS)
    ]
    operands = [got] * tiles + [shared, shared]
    aliases = {}
    if result is not None:
        in_specs.append(pl.BlockSpec(memory_space=pl.ANY))
        aliases = {3 + len(operands): 0}
        operands.append(result)
    pairs = heads * PER_GROUP * rows * length
    return pl.pallas_call(
        functools.partial(attend_kernel, tiles=tiles, docs=lengths.shape[0]),
        out_shape=jax.ShapeDtypeStruct((rows, QUERY_HEADS * HEAD_SIZE), jnp.bfloat16),
        grid_spec=pltpu.PrefetchScalarGridSpec(
            num_scalar_prefetch=3,
            grid=(heads,),
            in_specs=in_specs,
            out_specs=pl.BlockSpec((rows, HEAD_WIDTH), lambda h, t, e, n: (0, first + h)),
            scratch_shapes=[pltpu.VMEM((rows, length), jnp.float32)],
        ),
        input_output_aliases=aliases,
        compiler_params=pltpu.CompilerParams(vmem_limit_bytes=40 * 2**20),
        cost_estimate=pl.CostEstimate(
            flops=4 * pairs * HEAD_SIZE, bytes_accessed=4 * rows * heads * HEAD_WIDTH, transcendentals=pairs
        ),
    )(take, lengths, info, *operands)


def local(queries, keys, values, doc_lengths, send_tile, take_slot):
    tok_rows = queries.shape[0]
    peer_count = lax.axis_size("cp")
    tile_rows = tok_rows // peer_count
    chosen, placed = send_tile[0], take_slot[0]
    kv_width = KEY_VALUE_HEADS * HEAD_SIZE

    def exchange(source):
        return lax.all_to_all(source, "cp", split_axis=0, concat_axis=0, tiled=True)

    info = (lax.axis_index("grp") * tok_rows).astype(jnp.int32).reshape(1)
    early, late = PARTS
    sources, blocks = [keys, values] + [queries] * early, [0, 0] + list(range(early))
    got = exchange(pack(chosen, sources, blocks, tile_rows, HEAD_WIDTH))
    sources, blocks = [queries] * late, list(range(early, early + late))
    packed = pack(chosen, sources, blocks, tile_rows, HEAD_WIDTH)
    packed, got = lax.optimization_barrier((packed, got))
    rest = exchange(packed)
    received = got.reshape(-1, got.shape[2])
    owned = pack(placed, [received], [0], tile_rows, 2 * kv_width).reshape(tok_rows, 2 * kv_width)
    shared = lax.all_gather(owned, "grp", axis=0, tiled=True)
    lengths, skip = doc_lengths[0], 2 * kv_width // HEAD_WIDTH
    result = attend(placed, lengths, info, got, shared, None, 0, early, skip)
    return attend(placed, lengths, info, rest, shared, result, early, late, 0)


def solution(mesh):
    both = P(("cp", "grp"), None)
    return jax.shard_map(
        local,
        mesh=mesh,
        in_specs=(both, both, both, P("cp", None), both, both),
        out_specs=both,
        check_vma=False,
    )
```
